512 devices in a mesh: head: 8 (over x, z_lo), ctx: 64 (over z_hi, y, core).
Axes of the slice: x: 4, y: 8, z: 8 (z_hi: 4, z_lo: 2; z = z_hi * 2 + z_lo), core: 2. Of those that a mesh axis runs over, the one named last changes fastest.
Arguments:
- queries: bfloat16 [65536, 3072], P(('ctx', 'head')), may hold values from -6 to 6
- key_states: bfloat16 [65536, 3072], P(('ctx', 'head')), may hold values from -6 to 6
- value_states: bfloat16 [65536, 3072], P(('ctx', 'head')), may hold values from -6 to 6
- doc_ids: int32 [65536], replicated, may hold values from 0 to 31, never falling along the last dimension, each value on 1 to 4096 neighbouring positions
Outputs:
- attended: bfloat16 [65536, 3072], P(('ctx', 'head'))
The draws below stay inside these ranges and needn't reach their ends.
Inputs may be any that keep to these rules, and one draw needn't show every extreme that they name: `doc_ids`: non-decreasing along the sequence; every document holds 1 to 4096 positions and one holds exactly 4096.
All inputs are finite; a program needn't handle non-finite values.
Results may differ from the reference program's by a relative error of at most 0.006.
Values may be sent and summed in bfloat16 or wider, within the bound.
No kernel may reach another device: no remote copies, remote signals or barrier semaphores. Data moves between devices by JAX's collectives and lax.ppermute only.
A program may use at most 128 MiB of HBM per device.

```python
import math
import jax
import jax.numpy as jnp
import numpy as np
from jax import lax

HEADS = 24
HD = 128
STEPS = 3
BLOCK = 1024
TOKENS = 65536
DOCS = 32
DOC_MOST = 4096
N_CTX = 64


def draw_queries(key, part):
    key = jax.random.fold_in(key, 1)
    return jnp.clip(jax.random.normal(key, (TOKENS, HEADS * HD), dtype=jnp.float32), -6.0, 6.0).astype(jnp.bfloat16)


def draw_key_states(key, part):
    key = jax.random.fold_in(key, 2)
    return jnp.clip(jax.random.normal(key, (TOKENS, HEADS * HD), dtype=jnp.float32), -6.0, 6.0).astype(jnp.bfloat16)


def shard_levels(stream_key, dims, split, smallest, high):
    gain, own = 1.0, jax.random.fold_in(stream_key, 6)
    for dim, blocks in split:
        steps = jnp.exp(jax.random.uniform(jax.random.fold_in(own, dim), (blocks,), jnp.float32, smallest / len(split), high / len(split)))
        gain = gain * jnp.repeat(steps, dims[dim] // blocks).reshape([-1 if axis == dim else 1 for axis in range(len(dims))])
    return gain


def split_up(count, total, limit, slope):
    loads = [(1 << 20) // math.isqrt(standing ** slope) + 1 for standing in range(2, count + 1)]
    rest, counts = total - limit - (count - 1), [1] * (count - 1)
    while rest > 0:
        free = [i for i in range(count - 1) if counts[i] < limit]
        mass, left = sum([loads[i] for i in free]), rest
        for i in free:
            extra = min(limit - counts[i], max(1, left * loads[i] // mass), rest)
            counts[i] = counts[i] + extra
            rest = rest - extra
    return np.array([limit] + counts)


def ragged_sizes(own_key, count, total, reach, skew):
    if count == 2:
        one = jax.random.randint(own_key, (), max(1, total - reach), min(reach, total - 1) + 1)
        return jnp.stack([one, total - one])
    tallies = jnp.asarray(split_up(count, total, reach, skew), jnp.int32)
    twos = (count - 1) // 2
    giver, receiver = tallies[1:1 + 2 * twos:2], tallies[2:2 + 2 * twos:2]
    margin = jnp.minimum(giver - 1, reach - receiver)
    passed = jax.random.randint(jax.random.fold_in(own_key, 1), (twos,), 0, 1 << 20) % (margin + 1)
    tallies = tallies.at[1:1 + 2 * twos:2].set(giver - passed).at[2:2 + 2 * twos:2].set(receiver + passed)
    return tallies[jax.random.permutation(jax.random.fold_in(own_key, 2), count)]


def scatter_about(rng, shape, scale, reach, cuts=(), kind=jnp.bfloat16):
    result = jax.random.normal(rng, shape, jnp.float32) * scale
    if len(cuts) > 0:
        result = shard_levels(rng, shape, cuts, -0.22, 0.18) * result
    return jnp.clip(result, min=-reach, max=reach).astype(kind)


def setup_inputs(seed: int = 0) -> dict:
    splits = jax.random.split(jax.random.key(seed), 5)
    return {
        "queries": draw_queries(jax.random.fold_in(splits[4], 71), 0),
        "key_states": draw_key_states(jax.random.fold_in(splits[4], 71), 0),
        "value_states": scatter_about(splits[2], (TOKENS, HEADS * HD), 1.0, 6.0, ((0, 512),)),
        "doc_ids": jnp.searchsorted(jnp.cumsum(ragged_sizes(splits[3], DOCS, TOKENS, DOC_MOST, 0)), jnp.arange(TOKENS), side="right").astype(jnp.int32),
    }


masked_low = -1.0e30


def block_terms(query_block, key_block, value_block, query_docs, key_docs, query_pos, key_pos, present):
    scores = jnp.einsum("qhd,khd->qhk", query_block.astype(jnp.float32), key_block.astype(jnp.float32)) * (HD ** -0.5)
    allowed = (query_docs[:, None] == key_docs[None, :]) & (key_pos[None, :] <= query_pos[:, None]) & present
    allowed = allowed[:, None, :]
    scores = jnp.where(allowed, scores, masked_low)
    block_max = jnp.max(scores, axis=2)
    weights = jnp.where(allowed, jnp.exp(scores - block_max[:, :, None]), 0.0).astype(jnp.bfloat16)
    block_sum = jnp.sum(weights.astype(jnp.float32), axis=2)
    block_out = jnp.einsum("qhk,khd->qhd", weights.astype(jnp.float32), value_block.astype(jnp.float32))
    return block_out, block_max, block_sum


def merge_terms(terms):
    row_top = terms[0][1]
    for each_term in terms[1:]:
        row_top = jnp.maximum(row_top, each_term[1])
    numer = jnp.zeros_like(terms[0][0])
    denom = jnp.zeros_like(terms[0][2])
    for block_out, block_max, block_sum in terms:
        factor = jnp.exp(block_max - row_top)
        numer = numer + factor[:, :, None] * block_out
        denom = denom + factor * block_sum
    return numer / denom[:, :, None]


def reference(queries, key_states, value_states, doc_ids):
    shaped = (N_CTX, BLOCK, HEADS, HD)
    query_blocks = queries.reshape(shaped)
    key_blocks = key_states.reshape(shaped)
    value_blocks = value_states.reshape(shaped)
    doc_blocks = doc_ids.reshape(N_CTX, BLOCK)
    positions = jnp.arange(TOKENS, dtype=jnp.int32).reshape(N_CTX, BLOCK)

    def one_block(index):
        terms = []
        for offset in range(STEPS):
            source = jnp.maximum(index - offset, 0).astype(jnp.int32)
            terms.append(block_terms(query_blocks[index], key_blocks[source], value_blocks[source],
                                     doc_blocks[index], doc_blocks[source], positions[index],
                                     positions[source], index >= offset))
        return merge_terms(terms).astype(jnp.bfloat16)

    attended = lax.map(one_block, jnp.arange(N_CTX, dtype=jnp.int32))
    return attended.reshape(TOKENS, HEADS * HD)
```

```python
import functools

import jax
import jax.numpy as jnp
from jax import lax
from jax.experimental import pallas as pl
from jax.experimental.pallas import tpu as pltpu
from jax.sharding import PartitionSpec as P

HEADS = 24
HD = 128
BLOCK = 1024
ROWS = 128
GROUP = 8
WIDTH = 384
TILE = 256
LOW = -1e30
EXP_SCALE = HD**-0.5 * 1.4426950408889634
BF16 = jnp.bfloat16
F32 = jnp.float32


def vmem(mib=40):
    return pltpu.CompilerParams(vmem_limit_bytes=mib << 20)


def pack_kernel(*refs):
    in_refs, out_ref, sems = refs[:-2], refs[-2], refs[-1]
    copies = [
        pltpu.make_async_copy(
            ref.at[:, pl.ds(g * WIDTH, WIDTH)], out_ref.at[g, j], sems.at[j * GROUP + g]
        )
        for j, ref in enumerate(in_refs)
        for g in range(GROUP)
    ]
    for copy in copies:
        copy.start()
    for copy in copies:
        copy.wait()


def pack(name, *arrays):
    many = len(arrays)
    return pl.pallas_call(
        pack_kernel,
        in_specs=[pl.BlockSpec(memory_space=pl.ANY)] * many,
        out_specs=VM,
        out_shape=jax.ShapeDtypeStruct((GROUP, many, ROWS, WIDTH), BF16),
        scratch_shapes=[pltpu.SemaphoreType.DMA((many * GROUP,))],
        compiler_params=vmem(60),
        name=name,
    )(*arrays)


def unpack_kernel(in_ref, out_ref):
    for g in range(GROUP):
        out_ref[:, g * WIDTH : (g + 1) * WIDTH] = in_ref[g]


def unpack(slabs):
    return pl.pallas_call(
        unpack_kernel,
        in_specs=[VM],
        out_specs=VM,
        out_shape=jax.ShapeDtypeStruct((ROWS, HEADS * HD), BF16),
        compiler_params=vmem(8),
        name="unpack",
    )(slabs)


def scores_of(q, k):
    return lax.dot_general(q, k, (((1,), (1,)), ((), ())), preferred_element_type=F32)


def widen(v):
    return jnp.concatenate([v, jnp.ones_like(v)], axis=1)


def weigh(p, v):
    return jnp.dot(p, widen(v), preferred_element_type=F32)


def tiles():
    return [(slice(i * TILE, (i + 1) * TILE), i) for i in range(BLOCK // TILE)]


def rows_of(ref):
    return ref[...].reshape(BLOCK, HD)


def own_kernel(q_ref, k_ref, v_ref, dq_ref, dk_ref, o_ref, m_ref):
    q_all, k, v = rows_of(q_ref), rows_of(k_ref), rows_of(v_ref)
    for r, i in tiles():
        n = (i + 1) * TILE
        s = scores_of(q_all[r], k[:n])
        row = lax.broadcasted_iota(jnp.int32, (TILE, n), 0) + i * TILE
        col = lax.broadcasted_iota(jnp.int32, (TILE, n), 1)
        s = jnp.where((dq_ref[r, :] == dk_ref[:, :n]) & (row >= col), s, LOW)
        m = jnp.max(s, axis=1, keepdims=True)
        p = jnp.exp2((s - m) * EXP_SCALE).astype(BF16)
        o_ref[r, :] = weigh(p, v[:n])
        m_ref[r, :] = jnp.broadcast_to(m, (TILE, HD))


def score_kernel(q_ref, direct_ref, relay_ref, near_ref, dq_ref, dfar_ref, dnear_ref, o_ref, m_ref,
                 onew_ref, pfar_ref, pnear_ref):
    q_all, near = rows_of(q_ref), rows_of(near_ref)
    far = rows_of(direct_ref) + rows_of(relay_ref)
    for r, i in tiles():
        q, dq = q_all[r], dq_ref[r, :]
        s = jnp.where(dq == dfar_ref[...], scores_of(q, far), LOW)
        t = jnp.where(dq == dnear_ref[...], scores_of(q, near), LOW)
        m0 = m_ref[r, :1]
        m = jnp.maximum(
            jnp.maximum(jnp.max(s, axis=1, keepdims=True), jnp.max(t, axis=1, keepdims=True)), m0
        )
        pfar_ref[0, r, :] = jnp.exp2((s - m) * EXP_SCALE).astype(BF16)
        pnear_ref[0, r, :] = jnp.exp2((t - m) * EXP_SCALE).astype(BF16)
        onew_ref[r, :] = o_ref[r, :] * jnp.exp2((m0 - m) * EXP_SCALE)


def far_kernel(p_ref, direct_ref, relay_ref, o_ref, onew_ref):
    v = rows_of(direct_ref) + rows_of(relay_ref)
    for r, _ in tiles():
        onew_ref[r, :] = o_ref[r, :] + weigh(p_ref[0, r, :], v)


def near_kernel(p_ref, v_ref, o_ref, out_ref):
    v = rows_of(v_ref)
    for r, i in tiles():
        o = o_ref[r, :] + weigh(p_ref[0, r, :], v)
        out_ref[2 * i : 2 * i + 2] = (o[:, :HD] / o[:, HD:]).astype(BF16).reshape(2, ROWS, HD)


VM = pl.BlockSpec(memory_space=pltpu.VMEM)
SLAB = pl.BlockSpec((GROUP, ROWS, HD), lambda h: (0, 0, h))
COL = pl.BlockSpec((BLOCK, 1), lambda h: (0, 0))
ROW = pl.BlockSpec((1, BLOCK), lambda h: (0, 0))
SUMS = pl.BlockSpec((BLOCK, 2 * HD), lambda h: (0, h))
TOPS = pl.BlockSpec((BLOCK, HD), lambda h: (0, h))
WEIGHTS = pl.BlockSpec((1, BLOCK, BLOCK), lambda h: (h, 0, 0))
SLAB_T = jax.ShapeDtypeStruct((GROUP, ROWS, WIDTH), BF16)
SUMS_T = jax.ShapeDtypeStruct((BLOCK, 2 * WIDTH), F32)
TOPS_T = jax.ShapeDtypeStruct((BLOCK, WIDTH), F32)
WEIGHTS_T = jax.ShapeDtypeStruct((3, BLOCK, BLOCK), BF16)


def call(name, body, ins, outs, shapes, matmuls, exps, mib=24):
    return pl.pallas_call(
        body,
        grid=(3,),
        in_specs=ins,
        out_specs=outs,
        out_shape=shapes,
        compiler_params=vmem(mib),
        cost_estimate=pl.CostEstimate(
            flops=int(matmuls * 3 * BLOCK * BLOCK),
            bytes_accessed=1 << 18,
            transcendentals=int(exps * 3 * BLOCK),
        ),
        name=name,
    )


def exchange(slabs):
    return lax.all_to_all(slabs, "head", split_axis=0, concat_axis=0, tiled=True)


def routes():
    at = lambda head, block: head * 64 + block
    via = {(0, 0): 7, (0, 1): 1, (1, 1): 6}
    direct, out, back = [], [], []
    for head in range(GROUP):
        for block in range(62):
            run, core, z_lo = block // 16, block % 2, head % 2
            if block % 16 < 14 or (z_lo, core) not in via:
                direct.append((at(head, block), at(head, block + 2)))
            else:
                stop = at(head, (run + 1) * 16 + via[z_lo, core] * 2 + core)
                out.append((at(head, block), stop))
                back.append((stop, at(head, block + 2)))
    return direct, out, back


def local(queries, key_states, value_states, doc_ids):
    blocks = lax.axis_size("ctx")
    here = lax.axis_index("ctx")
    even = here % 2 == 0
    docs = doc_ids.reshape(blocks, BLOCK)

    def docs_of(back):
        ids = lax.dynamic_slice_in_dim(docs, jnp.maximum(here - back, 0), 1)
        return jnp.where(here >= back, ids, -1)

    down, dnear, dfar = docs_of(0), docs_of(1), docs_of(2)
    dq = down.reshape(BLOCK, 1)
    direct_pairs, out_pairs, back_pairs = routes()
    swap = [(i, i ^ 1) for i in range(blocks)]
    axes = ("head", "ctx")

    def far_of(own):
        direct = lax.ppermute(own, axes, direct_pairs)
        relay = lax.ppermute(lax.ppermute(own, axes, out_pairs), axes, back_pairs)
        return direct, relay

    def near_of(own, direct, relay, after):
        mine, after = lax.optimization_barrier((jnp.where(even, own, direct + relay), after))
        return lax.ppermute(mine, "ctx", swap), after

    k = exchange(pack("pack_k", key_states))[:, 0]
    k_direct, k_relay = far_of(k)
    vq = exchange(pack("pack_vq", value_states, queries))
    v, q = vq[:, 0], vq[:, 1]
    v, _ = lax.optimization_barrier((v, k_direct))
    v_direct, v_relay = far_of(v)
    o, m = call(
        "own", own_kernel, [SLAB] * 3 + [COL, ROW], [SUMS, TOPS], [SUMS_T, TOPS_T], 1, 1
    )(q, k, v, dq, down)
    k_near, m = near_of(k, k_direct, k_relay, m)
    o, p_far, p_near = call(
        "score", score_kernel, [SLAB] * 4 + [COL, ROW, ROW, SUMS, TOPS], [SUMS, WEIGHTS, WEIGHTS],
        [SUMS_T, WEIGHTS_T, WEIGHTS_T], 1, 2,
    )(q, k_direct, k_relay, k_near, dq, dfar, dnear, o, m)
    v_near, o = near_of(v, v_direct, v_relay, o)
    o = call("far", far_kernel, [WEIGHTS, SLAB, SLAB, SUMS], SUMS, SUMS_T, 0.5, 0)(
        p_far, v_direct, v_relay, o
    )
    out = call("near", near_kernel, [WEIGHTS, SLAB, SUMS], SLAB, SLAB_T, 0.5, 0)(p_near, v_near, o)
    return unpack(exchange(out))


def solution(mesh):
    rows = P(("ctx", "head"), None)
    return jax.shard_map(
        local,
        mesh=mesh,
        in_specs=(rows, rows, rows, P()),
        out_specs=rows,
        check_vma=False,
    )
```

```python
import functools

import jax
import jax.numpy as jnp
from jax import lax
from jax.experimental import pallas as pl
from jax.experimental.pallas import tpu as pltpu
from jax.sharding import PartitionSpec as P

HEADS = 24
HD = 128
DOCS = 32
BLOCK = 1024
ROWS = 128
GROUP = 8
WIDTH = 384
TILE = 256
LOW = -1e30
EXP_SCALE = HD**-0.5 * 1.4426950408889634
BF16 = jnp.bfloat16
F32 = jnp.float32


def vmem(mib=40):
    return pltpu.CompilerParams(vmem_limit_bytes=mib << 20)


def pack_kernel(*refs):
    in_refs, out_ref, sems = refs[:-2], refs[-2], refs[-1]
    copies = [
        pltpu.make_async_copy(
            ref.at[:, pl.ds(g * WIDTH, WIDTH)], out_ref.at[g, j], sems.at[j * GROUP + g]
        )
        for j, ref in enumerate(in_refs)
        for g in range(GROUP)
    ]
    for copy in copies:
        copy.start()
    for copy in copies:
        copy.wait()


def pack(name, *arrays):
    many = len(arrays)
    return pl.pallas_call(
        pack_kernel,
        in_specs=[pl.BlockSpec(memory_space=pl.ANY)] * many,
        out_specs=VM,
        out_shape=jax.ShapeDtypeStruct((GROUP, many, ROWS, WIDTH), BF16),
        scratch_shapes=[pltpu.SemaphoreType.DMA((many * GROUP,))],
        compiler_params=vmem(60),
        name=name,
    )(*arrays)


def unpack_kernel(in_ref, out_ref):
    for g in range(GROUP):
        out_ref[:, g * WIDTH : (g + 1) * WIDTH] = in_ref[g]


def unpack(slabs):
    return pl.pallas_call(
        unpack_kernel,
        in_specs=[VM],
        out_specs=VM,
        out_shape=jax.ShapeDtypeStruct((ROWS, HEADS * HD), BF16),
        compiler_params=vmem(8),
        name="unpack",
    )(slabs)


def scores_of(q, k):
    return lax.dot_general(q, k, (((1,), (1,)), ((), ())), preferred_element_type=F32)


def widen(v):
    return jnp.concatenate([v, jnp.ones_like(v)], axis=1)


def weigh(p, v):
    return jnp.dot(p, widen(v), preferred_element_type=F32)


def tiles():
    return [(slice(i * TILE, (i + 1) * TILE), i) for i in range(BLOCK // TILE)]


def rows_of(ref, which):
    return ref[:, which].reshape(BLOCK, HD)


def state_of(o, m):
    lane = lax.broadcasted_iota(jnp.int32, (TILE, HD), 1)
    return o[:, :HD], jnp.where(lane < HD // 2, m, o[:, HD:])


def own_kernel(q_ref, kv_ref, tq_ref, tk_ref, o_ref, st_ref):
    q_all = jnp.concatenate([rows_of(q_ref, 0), tq_ref[...]], axis=1)
    k = jnp.concatenate([rows_of(kv_ref, 0), tk_ref[...]], axis=1)
    v = rows_of(kv_ref, 1)
    row = lax.broadcasted_iota(jnp.int32, (TILE, TILE), 0)
    col = lax.broadcasted_iota(jnp.int32, (TILE, TILE), 1)
    for r, i in tiles():
        past, n = i * TILE, (i + 1) * TILE
        parts = [jnp.where(row >= col, scores_of(q_all[r], k[past:n]), LOW)]
        if past:
            parts.insert(0, scores_of(q_all[r], k[:past]))
        m = functools.reduce(jnp.maximum, [jnp.max(s, axis=1, keepdims=True) for s in parts])
        p = jnp.concatenate([jnp.exp2((s - m) * EXP_SCALE).astype(BF16) for s in parts], axis=1)
        o_ref[r, :], st_ref[r, :] = state_of(weigh(p, v[:n]), m)


def later_kernel(final, parts, q_ref, *refs):
    kv_refs, (tq_ref, tk_ref, oi_ref, sti_ref) = refs[:parts], refs[parts : parts + 4]
    outs = refs[parts + 4 :]
    k, v = [sum((rows_of(ref, j) for ref in kv_refs[1:]), rows_of(kv_refs[0], j)) for j in (0, 1)]
    q_all = jnp.concatenate([rows_of(q_ref, 0), tq_ref[...]], axis=1)
    k = jnp.concatenate([k, tk_ref[...]], axis=1)
    for r, i in tiles():
        s = scores_of(q_all[r], k)
        st = sti_ref[r, :]
        m0, l0 = st[:, :1], st[:, HD // 2 : HD // 2 + 1]
        m = jnp.maximum(m0, jnp.max(s, axis=1, keepdims=True))
        o = weigh(jnp.exp2((s - m) * EXP_SCALE).astype(BF16), v)
        back = jnp.exp2((m0 - m) * EXP_SCALE)
        o = jnp.concatenate([o[:, :HD] + oi_ref[r, :] * back, o[:, HD:] + l0 * back], axis=1)
        if final:
            out = (o[:, :HD] / o[:, HD:]).astype(BF16)
            slabs = TILE // ROWS
            outs[0][slabs * i : slabs * (i + 1)] = out.reshape(slabs, ROWS, HD)
        else:
            outs[0][r, :], outs[1][r, :] = state_of(o, m)


VM = pl.BlockSpec(memory_space=pltpu.VMEM)
ONE = pl.BlockSpec((GROUP, 1, ROWS, HD), lambda h: (0, 0, 0, h))
TWO = pl.BlockSpec((GROUP, 2, ROWS, HD), lambda h: (0, 0, 0, h))
TAGS = pl.BlockSpec((BLOCK, HD), lambda h: (0, 0))
STATE = pl.BlockSpec((BLOCK, HD), lambda h: (0, h))
OUT = pl.BlockSpec((GROUP, ROWS, HD), lambda h: (0, 0, h))
STATE_T = jax.ShapeDtypeStruct((BLOCK, WIDTH), F32)
OUT_T = jax.ShapeDtypeStruct((GROUP, ROWS, WIDTH), BF16)


def call(name, body, ins, outs, shapes):
    return pl.pallas_call(
        body,
        grid=(3,),
        in_specs=ins,
        out_specs=outs,
        out_shape=shapes,
        compiler_params=vmem(24),
        cost_estimate=pl.CostEstimate(
            flops=BLOCK * BLOCK, bytes_accessed=1 << 18, transcendentals=BLOCK
        ),
        name=name,
    )


def exchange(slabs):
    return lax.all_to_all(slabs, "head", split_axis=0, concat_axis=0, tiled=True)


def routes():
    at = lambda head, block: head * 64 + block
    via = {(0, 0): 7, (0, 1): 1}
    pairs = {name: [] for name in ("direct", "out", "back", "up", "down", "down_relayed")}
    for head in range(GROUP):
        for block in range(64):
            run, core, z_lo = block // 16, block % 2, head % 2
            if core == 0:
                pairs["up"].append((at(head, block), at(head, block + 1)))
            else:
                came = block % 16 == 1 and run > 0 and (z_lo, core) in via
                name = "down_relayed" if came else "down"
                pairs[name].append((at(head, block), at(head, block - 1)))
            if block >= 62:
                continue
            if block % 16 < 14 or (z_lo, core) not in via:
                pairs["direct"].append((at(head, block), at(head, block + 2)))
            else:
                stop = at(head, (run + 1) * 16 + via[z_lo, core] * 2 + core)
                pairs["out"].append((at(head, block), stop))
                pairs["back"].append((stop, at(head, block + 2)))
    return pairs


def local(queries, key_states, value_states, doc_ids):
    blocks = lax.axis_size("ctx")
    here = lax.axis_index("ctx")
    docs = doc_ids.reshape(blocks, BLOCK)

    kinds = lax.broadcasted_iota(jnp.int32, (BLOCK, HD), 1)

    def docs_of(back):
        return lax.dynamic_slice_in_dim(docs, jnp.maximum(here - back, 0), 1).reshape(BLOCK, 1)

    def key_tags(back):
        ids = jnp.where(here >= back, docs_of(back), DOCS)
        return (ids == kinds).astype(BF16)

    down, dnear, dfar = key_tags(0), key_tags(1), key_tags(2)
    dq = jnp.where(docs_of(0) == kinds, 0.0, LOW).astype(BF16)
    pairs = routes()
    send = lambda array, name: lax.ppermute(array, ("head", "ctx"), pairs[name])

    kv = exchange(pack("pack_kv", key_states, value_states))
    q = exchange(pack("pack_q", queries))
    direct = send(kv, "direct")
    relay = send(send(kv, "out"), "back")
    near_up = send(kv, "up")
    o, st = call("own", own_kernel, [ONE, TWO, TAGS, TAGS], [STATE] * 2, [STATE_T] * 2)(
        q, kv, dq, down
    )
    direct, st = lax.optimization_barrier((direct, st))
    near_down = send(direct, "down")
    near_relayed = send(relay, "down_relayed")
    o, st = call(
        "far", functools.partial(later_kernel, False, 2), [ONE, TWO, TWO, TAGS, TAGS, STATE, STATE],
        [STATE] * 2, [STATE_T] * 2,
    )(q, direct, relay, dq, dfar, o, st)
    out = call(
        "near", functools.partial(later_kernel, True, 3), [ONE] + [TWO] * 3 + [TAGS, TAGS, STATE, STATE],
        OUT, OUT_T,
    )(q, near_up, near_down, near_relayed, dq, dnear, o, st)
    return unpack(exchange(out))


def solution(mesh):
    rows = P(("ctx", "head"), None)
    return jax.shard_map(
        local,
        mesh=mesh,
        in_specs=(rows, rows, rows, P()),
        out_specs=rows,
        check_vma=False,
    )
```

```python
import functools

import jax
import jax.numpy as jnp
from jax import lax
from jax.experimental import pallas as pl
from jax.experimental.pallas import tpu as pltpu
from jax.sharding import PartitionSpec as P

HEADS = 24
HD = 128
DOCS = 32
BLOCK = 1024
ROWS = 128
GROUP = 8
WIDTH = 384
TILE = 256
LOW = -1e30
EXP_SCALE = HD**-0.5 * 1.4426950408889634
BF16 = jnp.bfloat16
F32 = jnp.float32


def vmem(mib=40):
    return pltpu.CompilerParams(vmem_limit_bytes=mib << 20)


def pack_kernel(*refs):
    in_refs, out_ref, sems = refs[:-2], refs[-2], refs[-1]
    copies = [
        pltpu.make_async_copy(
            ref.at[:, pl.ds(g * WIDTH, WIDTH)], out_ref.at[g, j], sems.at[j * GROUP + g]
        )
        for j, ref in enumerate(in_refs)
        for g in range(GROUP)
    ]
    for copy in copies:
        copy.start()
    for copy in copies:
        copy.wait()


def pack(name, mib, *arrays):
    many = len(arrays)
    return pl.pallas_call(
        pack_kernel,
        in_specs=[pl.BlockSpec(memory_space=pl.ANY)] * many,
        out_specs=VM,
        out_shape=jax.ShapeDtypeStruct((GROUP, many, ROWS, WIDTH), BF16),
        scratch_shapes=[pltpu.SemaphoreType.DMA((many * GROUP,))],
        compiler_params=vmem(mib),
        name=name,
    )(*arrays)


def unpack_kernel(in_ref, out_ref):
    for g in range(GROUP):
        out_ref[:, g * WIDTH : (g + 1) * WIDTH] = in_ref[g]


def unpack(slabs):
    return pl.pallas_call(
        unpack_kernel,
        in_specs=[VM],
        out_specs=VM,
        out_shape=jax.ShapeDtypeStruct((ROWS, HEADS * HD), BF16),
        compiler_params=vmem(8),
        name="unpack",
    )(slabs)


def scores_of(q, k):
    return lax.dot_general(q, k, (((1,), (1,)), ((), ())), preferred_element_type=F32)


def widen(v):
    return jnp.concatenate([v, jnp.ones_like(v)], axis=1)


def weigh(p, v):
    return jnp.dot(p, widen(v), preferred_element_type=F32)


def tiles():
    return [(slice(i * TILE, (i + 1) * TILE), i) for i in range(BLOCK // TILE)]


def rows_of(ref, which):
    return ref[:, which].reshape(BLOCK, HD)


def state_of(o, m):
    lane = lax.broadcasted_iota(jnp.int32, (TILE, HD), 1)
    return o[:, :HD], jnp.where(lane < HD // 2, m, o[:, HD:])


def own_kernel(q_ref, kv_ref, tq_ref, tk_ref, o_ref, st_ref):
    q_all = jnp.concatenate([rows_of(q_ref, 0), tq_ref[...]], axis=1)
    k = jnp.concatenate([rows_of(kv_ref, 0), tk_ref[...]], axis=1)
    v = rows_of(kv_ref, 1)
    row = lax.broadcasted_iota(jnp.int32, (TILE, TILE), 0)
    col = lax.broadcasted_iota(jnp.int32, (TILE, TILE), 1)
    for r, i in tiles():
        past, n = i * TILE, (i + 1) * TILE
        parts = [jnp.where(row >= col, scores_of(q_all[r], k[past:n]), LOW)]
        if past:
            parts.insert(0, scores_of(q_all[r], k[:past]))
        m = functools.reduce(jnp.maximum, [jnp.max(s, axis=1, keepdims=True) for s in parts])
        p = jnp.concatenate([jnp.exp2((s - m) * EXP_SCALE).astype(BF16) for s in parts], axis=1)
        o_ref[r, :], st_ref[r, :] = state_of(weigh(p, v[:n]), m)


def later_kernel(final, parts, q_ref, *refs):
    kv_refs, (tq_ref, tk_ref, oi_ref, sti_ref) = refs[:parts], refs[parts : parts + 4]
    outs = refs[parts + 4 :]
    for h in range(3):
        cols = slice(h * HD, (h + 1) * HD)
        rows = lambda ref, j: ref[:, j, :, cols].reshape(BLOCK, HD)
        k, v = [sum((rows(ref, j) for ref in kv_refs[1:]), rows(kv_refs[0], j)) for j in (0, 1)]
        q_all = jnp.concatenate([rows(q_ref, 0), tq_ref[...]], axis=1)
        k = jnp.concatenate([k, tk_ref[...]], axis=1)
        for r, i in tiles():
            s = scores_of(q_all[r], k)
            st = sti_ref[r, cols]
            m0, l0 = st[:, :1], st[:, HD // 2 : HD // 2 + 1]
            m = jnp.maximum(m0, jnp.max(s, axis=1, keepdims=True))
            o = weigh(jnp.exp2((s - m) * EXP_SCALE).astype(BF16), v)
            back = jnp.exp2((m0 - m) * EXP_SCALE)
            o = jnp.concatenate([o[:, :HD] + oi_ref[r, cols] * back, o[:, HD:] + l0 * back], axis=1)
            if final:
                out = (o[:, :HD] / o[:, HD:]).astype(BF16)
                slabs = TILE // ROWS
                outs[0][slabs * i : slabs * (i + 1), :, cols] = out.reshape(slabs, ROWS, HD)
            else:
                outs[0][r, cols], outs[1][r, cols] = state_of(o, m)


VM = pl.BlockSpec(memory_space=pltpu.VMEM)
ONE = pl.BlockSpec((GROUP, 1, ROWS, HD), lambda h: (0, 0, 0, h))
TWO = pl.BlockSpec((GROUP, 2, ROWS, HD), lambda h: (0, 0, 0, h))
TAGS = pl.BlockSpec((BLOCK, HD), lambda h: (0, 0))
STATE = pl.BlockSpec((BLOCK, HD), lambda h: (0, h))
OUT = pl.BlockSpec((GROUP, ROWS, HD), lambda h: (0, 0, h))
STATE_T = jax.ShapeDtypeStruct((BLOCK, WIDTH), F32)
OUT_T = jax.ShapeDtypeStruct((GROUP, ROWS, WIDTH), BF16)


def call(name, body, ins, outs, shapes):
    return pl.pallas_call(
        body,
        grid=(3,),
        in_specs=ins,
        out_specs=outs,
        out_shape=shapes,
        compiler_params=vmem(20),
        cost_estimate=pl.CostEstimate(
            flops=BLOCK * BLOCK, bytes_accessed=1 << 18, transcendentals=BLOCK
        ),
        name=name,
    )


def whole(name, body, count, outs, shapes):
    return pl.pallas_call(
        body,
        in_specs=[VM] * count,
        out_specs=outs,
        out_shape=shapes,
        compiler_params=vmem(20),
        cost_estimate=pl.CostEstimate(
            flops=BLOCK * BLOCK, bytes_accessed=1 << 18, transcendentals=BLOCK
        ),
        name=name,
    )


def exchange(slabs):
    return lax.all_to_all(slabs, "head", split_axis=0, concat_axis=0, tiled=True)


def routes():
    at = lambda head, block: head * 64 + block
    via = {(0, 0): 7, (0, 1): 1}
    pairs = {name: [] for name in ("direct", "out", "back", "up", "down", "down_relayed")}
    for head in range(GROUP):
        for block in range(64):
            run, core, z_lo = block // 16, block % 2, head % 2
            if core == 0:
                pairs["up"].append((at(head, block), at(head, block + 1)))
            else:
                came = block % 16 == 1 and run > 0 and (z_lo, core) in via
                name = "down_relayed" if came else "down"
                pairs[name].append((at(head, block), at(head, block - 1)))
            if block >= 62:
                continue
            if block % 16 < 14 or (z_lo, core) not in via:
                pairs["direct"].append((at(head, block), at(head, block + 2)))
            else:
                stop = at(head, (run + 1) * 16 + via[z_lo, core] * 2 + core)
                pairs["out"].append((at(head, block), stop))
                pairs["back"].append((stop, at(head, block + 2)))
    return pairs


def local(queries, key_states, value_states, doc_ids):
    blocks = lax.axis_size("ctx")
    here = lax.axis_index("ctx")
    docs = doc_ids.reshape(blocks, BLOCK)

    kinds = lax.broadcasted_iota(jnp.int32, (BLOCK, HD), 1)

    def docs_of(back):
        return lax.dynamic_slice_in_dim(docs, jnp.maximum(here - back, 0), 1).reshape(BLOCK, 1)

    def key_tags(back):
        ids = jnp.where(here >= back, docs_of(back), DOCS)
        return (ids == kinds).astype(BF16)

    down, dnear, dfar = key_tags(0), key_tags(1), key_tags(2)
    dq = jnp.where(docs_of(0) == kinds, 0.0, LOW).astype(BF16)
    pairs = routes()
    send = lambda array, name: lax.ppermute(array, ("head", "ctx"), pairs[name])

    kv = exchange(pack("pack_kv", 60, key_states, value_states))
    q = exchange(pack("pack_q", 8, queries))
    direct = send(kv, "direct")
    relay = send(send(kv, "out"), "back")
    near_up = send(kv, "up")
    o, st = call("own", own_kernel, [ONE, TWO, TAGS, TAGS], [STATE] * 2, [STATE_T] * 2)(
        q, kv, dq, down
    )
    direct, st = lax.optimization_barrier((direct, st))
    near_down = send(direct, "down")
    near_relayed = send(relay, "down_relayed")
    far = functools.partial(later_kernel, False, 2)
    o, st = whole("far", far, 7, [VM] * 2, [STATE_T] * 2)(q, direct, relay, dq, dfar, o, st)
    near = functools.partial(later_kernel, True, 3)
    out = whole("near", near, 8, VM, OUT_T)(
        q, near_up, near_down, near_relayed, dq, dnear, o, st
    )
    return unpack(exchange(out))


def solution(mesh):
    rows = P(("ctx", "head"), None)
    return jax.shard_map(
        local,
        mesh=mesh,
        in_specs=(rows, rows, rows, P()),
        out_specs=rows,
        check_vma=False,
    )
```
